32 devices in a mesh: rep: 4 (over x, core), hid: 8 (over z, y).
Axes of the slice: x: 2, y: 2, z: 4, core: 2. Of those that a mesh axis runs over, the one named last changes fastest.
Arguments:
- tokens: bfloat16 [1024, 8192], P('rep', 'hid'), may hold values from -6 to 6
- cotangent: bfloat16 [1024, 8192], P('rep', 'hid'), may hold values from -6 to 6
- seq_ids: int32 [4, 256], P('rep'), may hold values from 0 to 7, never falling along the last dimension, each value on 1 to 64 neighbouring positions
- in_blocks: int32 [128, 5], P('hid'), may hold values from 0 to 63, as said below
- out_blocks: int32 [128, 5], P('hid'), may hold values from 0 to 63, as said below
- unit_scale: float32 [16384], P('hid'), may hold values from 0.3 to 3.2
- gate_weight: bfloat16 [128, 5, 128, 128], P('hid'), may hold values from -6 to 6
- up_weight: bfloat16 [128, 5, 128, 128], P('hid'), may hold values from -6 to 6
- down_weight: bfloat16 [128, 5, 128, 128], P('hid'), may hold values from -6 to 6
Outputs:
- new_gate: bfloat16 [128, 5, 128, 128], P('hid')
- new_up: bfloat16 [128, 5, 128, 128], P('hid')
- new_down: bfloat16 [128, 5, 128, 128], P('hid')
The draws below stay inside these ranges and needn't reach their ends.
Inputs may be any that keep to these rules, and one draw needn't show every extreme that they name: `in_blocks`: each row lists 5 different blocks, and every block appears in some row. `out_blocks`: each row lists 5 different blocks, and every block appears in some row. `seq_ids`: ids never fall along a row; each sequence has 1 to 64 tokens.
All inputs are finite; a program needn't handle non-finite values.
Results may differ from the reference program's by a relative error of at most 0.0075.
Values may be sent and summed in bfloat16 or wider, within the bound.
A program may use at most 128 MiB of HBM per device.

```python
import math
import jax
import jax.numpy as jnp
import numpy as np
from jax import lax

D = 8192
FF = 16384
BLOCK = 128
LEVELS = 5
SEGS = 8
TOK_REP = 256
MOST_LEN = 64
NB_D = 64
NB_H = 128
TOKENS = 1024
N_REP = 4


def butterfly_rows(key):
    first, second = jax.random.split(key)
    block_perm = jax.random.permutation(first, NB_D)
    base = jax.random.permutation(second, NB_H) % NB_D
    strides = jnp.array([0, 1, 4, NB_D // 4, NB_D // 2], dtype=jnp.int32)
    position = jnp.bitwise_xor(base[:, None].astype(jnp.int32), strides[None, :])
    return block_perm[position].astype(jnp.int32)


def draw_in_blocks(key, part):
    return butterfly_rows(jax.random.fold_in(key, 101))


def draw_out_blocks(key, part):
    return butterfly_rows(jax.random.fold_in(key, 202))


def draw_unit_scale(key, part):
    inner = jax.random.fold_in(key, 303)
    ramp = jnp.arange(FF, dtype=jnp.float32) / FF
    rough = jax.random.uniform(inner, (FF,), jnp.float32, 0.75, 1.35)
    values = (0.6 + 1.2 * ramp) * rough
    return values.astype(jnp.float32)


def block_scale(own_key, dims, cuts, smallest, high):
    def one(dim, parts):
        steps = jax.random.uniform(jax.random.fold_in(jax.random.fold_in(own_key, 6), dim), (parts,), jnp.float32, smallest / len(cuts), high / len(cuts))
        return jnp.repeat(jnp.exp(steps), dims[dim] // parts).reshape((-1,) + (1,) * (len(dims) - dim - 1))

    factor_of = one(*cuts[0])
    for cut in cuts[1:]:
        factor_of = factor_of * one(*cut)
    return factor_of


def profile(number_of, total, bound, lean):
    loads = [(1 << 20) // math.isqrt(grade ** lean) + 1 for grade in range(2, number_of + 1)]
    spare, given = total - bound - (number_of - 1), [1] * (number_of - 1)
    while spare > 0:
        free = [i for i in range(number_of - 1) if given[i] < bound]
        mass, remaining = sum([loads[i] for i in free]), spare
        for i in free:
            more = min(bound - given[i], max(1, remaining * loads[i] // mass), spare)
            given[i] = given[i] + more
            spare = spare - more
    return np.array([bound] + given)


def ragged(stream_key, number_of, total, most, slope):
    if number_of == 2:
        one = jax.random.randint(stream_key, (), max(1, total - most), min(most, total - 1) + 1)
        return jnp.stack([one, total - one])
    lengths = jnp.asarray(profile(number_of, total, most, slope), jnp.int32)
    twos = (number_of - 1) // 2
    giver, receiver = lengths[1:1 + 2 * twos:2], lengths[2:2 + 2 * twos:2]
    slack = jnp.minimum(giver - 1, most - receiver)
    moved = jax.random.randint(jax.random.fold_in(stream_key, 1), (twos,), 0, 1 << 20) % (slack + 1)
    lengths = lengths.at[1:1 + 2 * twos:2].set(giver - moved).at[2:2 + 2 * twos:2].set(receiver + moved)
    return lengths[jax.random.permutation(jax.random.fold_in(stream_key, 2), number_of)]


def centred(rng, dims, deviation, reach, pieces=(), held_as=jnp.bfloat16):
    entries = deviation * jax.random.normal(rng, dims, jnp.float32)
    if pieces:
        entries = entries * block_scale(rng, dims, pieces, -0.22, 0.18)
    return jnp.clip(entries, -reach, reach).astype(held_as)


def setup_inputs(seed: int = 0) -> dict:
    streams_of = jax.random.split(jax.random.key(seed), 10)
    return {
        "tokens": centred(streams_of[0], (TOKENS, D), 1.0, 6.0, ((0, 4), (1, 8))),
        "cotangent": centred(streams_of[1], (TOKENS, D), 1.0, 6.0, ((0, 4), (1, 8))),
        "seq_ids": jax.vmap(lambda own: jnp.searchsorted(jnp.cumsum(ragged(own, SEGS, TOK_REP, MOST_LEN, 0)), jnp.arange(TOK_REP), side="right"))(jax.random.split(streams_of[2], N_REP)).reshape((N_REP, TOK_REP)).astype(jnp.int32),
        "in_blocks": draw_in_blocks(jax.random.fold_in(streams_of[9], 71), 0),
        "out_blocks": draw_out_blocks(jax.random.fold_in(streams_of[9], 71), 0),
        "unit_scale": draw_unit_scale(jax.random.fold_in(streams_of[9], 71), 0),
        "gate_weight": centred(streams_of[6], (NB_H, LEVELS, BLOCK, BLOCK), 1.0, 6.0, ((0, 8),)),
        "up_weight": centred(streams_of[7], (NB_H, LEVELS, BLOCK, BLOCK), 1.0, 6.0, ((0, 8),)),
        "down_weight": centred(streams_of[8], (NB_H, LEVELS, BLOCK, BLOCK), 1.0, 6.0, ((0, 8),)),
    }


learn_rate = 8.0
max_rms = 0.1

def replica_grads(tok_rows, cot_rows, seq_row, in_blocks, out_blocks, unit_scale, gate_weight, up_weight, down_weight):
    same_seq = (seq_row[:, None] == seq_row[None, :]).astype(jnp.float32)
    seq_len = lax.optimization_barrier(jnp.sum(same_seq, axis=1))
    tok_weight = TOK_REP / (SEGS * seq_len)
    scaled = (cot_rows.astype(jnp.float32) * tok_weight[:, None]).astype(jnp.bfloat16)
    hidden_blocks = FF // BLOCK
    in_scale = (LEVELS * BLOCK) ** (-0.5)
    out_scale = (LEVELS * BLOCK * (FF // D)) ** (-0.5)
    picked = jnp.take(tok_rows.reshape(TOK_REP, D // BLOCK, BLOCK), in_blocks.reshape(-1), axis=1)
    picked = picked.reshape(TOK_REP, hidden_blocks, LEVELS, BLOCK).astype(jnp.float32)
    gate_pre = jnp.einsum('thlc,hlcd->thd', picked, gate_weight.astype(jnp.float32)) * in_scale
    up_pre = jnp.einsum('thlc,hlcd->thd', picked, up_weight.astype(jnp.float32)) * in_scale
    unit_gain = unit_scale.reshape(hidden_blocks, BLOCK)
    sigmoid_gate = jax.nn.sigmoid(gate_pre)
    silu_gate = gate_pre * sigmoid_gate
    hidden = (silu_gate * up_pre * unit_gain).astype(jnp.bfloat16)
    picked_cot = jnp.take(scaled.reshape(TOK_REP, D // BLOCK, BLOCK), out_blocks.reshape(-1), axis=1)
    picked_cot = picked_cot.reshape(TOK_REP, hidden_blocks, LEVELS, BLOCK).astype(jnp.float32)
    d_hidden = jnp.einsum('thlo,hlio->thi', picked_cot, down_weight.astype(jnp.float32)) * out_scale
    grad_down = jnp.einsum('thi,thlo->hlio', hidden.astype(jnp.float32), picked_cot) * out_scale
    d_scaled = d_hidden * unit_gain
    d_gate = (d_scaled * up_pre * sigmoid_gate * (1.0 + gate_pre * (1.0 - sigmoid_gate))).astype(jnp.bfloat16)
    d_up = (d_scaled * silu_gate).astype(jnp.bfloat16)
    grad_gate = jnp.einsum('thlc,thd->hlcd', picked, d_gate.astype(jnp.float32)) * in_scale
    grad_up = jnp.einsum('thlc,thd->hlcd', picked, d_up.astype(jnp.float32)) * in_scale
    sq_total = jnp.sum(grad_gate * grad_gate) + jnp.sum(grad_up * grad_up) + jnp.sum(grad_down * grad_down)
    count_all = 3 * hidden_blocks * LEVELS * BLOCK * BLOCK
    rms_value = jnp.sqrt(sq_total / count_all + 1e-06)
    clip = jnp.minimum(1.0, max_rms / rms_value)
    step_size = -learn_rate * clip
    return (grad_gate * step_size, grad_up * step_size, grad_down * step_size)

def reference(tokens, cotangent, seq_ids, in_blocks, out_blocks, unit_scale, gate_weight, up_weight, down_weight):
    tok_split = tokens.reshape(N_REP, TOK_REP, D)
    cot_split = cotangent.reshape(N_REP, TOK_REP, D)

    def accumulate(carry, items):
        tok_rows, cot_rows, seq_row = items
        deltas = replica_grads(tok_rows, cot_rows, seq_row, in_blocks, out_blocks, unit_scale, gate_weight, up_weight, down_weight)
        return ((carry[0] + deltas[0], carry[1] + deltas[1], carry[2] + deltas[2]), None)
    shape = gate_weight.shape
    start = (jnp.zeros(shape, jnp.float32), jnp.zeros(shape, jnp.float32), jnp.zeros(shape, jnp.float32))
    totals, _ = lax.scan(accumulate, start, (tok_split, cot_split, seq_ids))
    new_gate = (gate_weight.astype(jnp.float32) + totals[0] / N_REP).astype(jnp.bfloat16)
    new_up = (up_weight.astype(jnp.float32) + totals[1] / N_REP).astype(jnp.bfloat16)
    new_down = (down_weight.astype(jnp.float32) + totals[2] / N_REP).astype(jnp.bfloat16)
    return (new_gate, new_up, new_down)
```

```python
import functools

import jax
import jax.numpy as jnp
from jax import lax
from jax.experimental import pallas as pl
from jax.experimental.pallas import tpu as pltpu
from jax.sharding import PartitionSpec as P

MESH = pl.DeviceIdType.MESH
F32 = jnp.float32
BF16 = jnp.bfloat16
SEGS = 8
LEARN_RATE = 8.0
MAX_RMS = 0.1
CORES = 2


def kernel(
    cfg,
    tok_hbm,
    cot_hbm,
    seq_ref,
    inb_ref,
    outb_ref,
    unit_ref,
    wg_hbm,
    wu_hbm,
    wd_hbm,
    og_hbm,
    ou_hbm,
    od_hbm,
    tokb,
    cotb,
    stage,
    wv,
    fac,
    hid_t,
    x_t,
    ggu,
    gdn,
    xb,
    sqb,
    load_sem,
    stage_sem,
    w_sem,
    ring_send,
    ring_recv,
    own_send,
    own_recv,
    core_send,
    core_recv,
    sq_send,
    sq_recv,
    x_send,
    x_recv,
    out_local,
    out_send,
    out_recv,
):
    G, R, T, bd, hb, L, B = (cfg[k] for k in ("G", "R", "T", "bd", "hb", "L", "B"))
    in_scale, out_scale, count_all = cfg["in_scale"], cfg["out_scale"], cfg["count_all"]
    peers = R // CORES
    half_ring = G // 2
    depth = G // 2
    hh = hb // CORES
    sub_n = bd // 2
    group = G * CORES

    rep, g = lax.axis_index("rep"), lax.axis_index("hid")
    c, p = lax.rem(rep, CORES), rep // CORES
    lin = g * CORES + c
    sib = (p * CORES + (1 - c), g)
    gy, gz = lax.rem(g, 2), g // 2
    pos = gz + gy * (2 * depth - 1 - 2 * gz)

    def ring_at(q):
        q = lax.rem(q + 2 * G, G)
        y, z = q // depth, lax.rem(q, depth)
        return (z + y * (depth - 1 - 2 * z)) * 2 + y

    right, left = (rep, ring_at(pos + 1)), (rep, ring_at(pos - 1))
    h0 = c * hh
    bufs = (tokb, cotb)

    w_copies = [
        pltpu.make_async_copy(src.at[pl.ds(h0, hh)], wv.at[j], w_sem.at[j])
        for j, src in enumerate((wg_hbm, wu_hbm, wd_hbm))
    ]
    tok_copies = [
        pltpu.make_async_copy(
            tok_hbm.at[:, pl.ds(b * B, B)], tokb.at[c, g * bd + b], load_sem.at[b]
        )
        for b in range(bd)
    ]
    cot_copy = pltpu.make_async_copy(cot_hbm, stage, stage_sem)
    for copy in tok_copies:
        copy.start()
    cot_copy.start()
    for copy in w_copies:
        copy.start()

    barrier = pltpu.get_barrier_semaphore()

    def greet(n, _):
        other = lax.rem(lin + n, group)
        pl.semaphore_signal(
            barrier,
            inc=1,
            device_id=(p * CORES + lax.rem(other, CORES), other // CORES),
            device_id_type=MESH,
        )
        return 0

    lax.fori_loop(1, group, greet, 0)
    for n in range(1, peers):
        pl.semaphore_signal(
            barrier,
            inc=1,
            device_id=(lax.rem(p + n, peers) * CORES + c, g),
            device_id_type=MESH,
        )
    pl.semaphore_wait(barrier, group - 1 + peers - 1)

    def blocks_of(k, origin, sub):
        return bufs[k].at[c, pl.ds(origin * bd + sub * sub_n, sub_n)]

    def ring_copy(way, s, k, sub):
        origin = ring_at(pos - (s - 1)) if way == 0 else ring_at(pos + (s - 1))
        ref = blocks_of(k, origin, sub)
        return pltpu.make_async_remote_copy(
            src_ref=ref,
            dst_ref=ref,
            send_sem=ring_send.at[way, s - 1, k, sub],
            recv_sem=ring_recv.at[way, s - 1, k, sub],
            device_id=right if way == 0 else left,
            device_id_type=MESH,
        )

    def ring_arrival(way, s, k, sub):
        origin = ring_at(pos - s) if way == 0 else ring_at(pos + s)
        ref = blocks_of(k, origin, sub)
        return pltpu.make_async_remote_copy(
            src_ref=ref,
            dst_ref=ref,
            send_sem=ring_send.at[way, s - 1, k, sub],
            recv_sem=ring_recv.at[way, s - 1, k, sub],
            device_id=right if way == 0 else left,
            device_id_type=MESH,
        )

    def in_step(way, s, sub):
        return s < half_ring or (s == half_ring and way == sub)

    def core_copy(way, s, k, sub, mine):
        origin = g if s == 0 else (ring_at(pos - s) if way == 0 else ring_at(pos + s))
        who = c if mine else 1 - c
        ref = bufs[k].at[who, pl.ds(origin * bd + sub * sub_n, sub_n)]
        if s == 0:
            sems = own_send.at[k, sub], own_recv.at[k, sub]
        else:
            sems = core_send.at[way, s - 1, k, sub], core_recv.at[way, s - 1, k, sub]
        return pltpu.make_async_remote_copy(
            src_ref=ref,
            dst_ref=ref,
            send_sem=sems[0],
            recv_sem=sems[1],
            device_id=sib,
            device_id_type=MESH,
        )

    def start_own(k):
        for sub in range(2):
            for way in range(2):
                if in_step(way, 1, sub):
                    ring_copy(way, 1, k, sub).start()
        for sub in range(2):
            core_copy(0, 0, k, sub, True).start()

    def serve(k, s):
        for sub in range(2):
            for way in range(2):
                if not in_step(way, s, sub):
                    continue
                ring_arrival(way, s, k, sub).wait_recv()
                if in_step(way, s + 1, sub):
                    ring_copy(way, s + 1, k, sub).start()
                core_copy(way, s, k, sub, True).start()

    def core_arrivals(k):
        for sub in range(2):
            core_copy(0, 0, k, sub, False).wait_recv()
            for s in range(1, half_ring + 1):
                for way in range(2):
                    if in_step(way, s, sub):
                        core_copy(way, s, k, sub, False).wait_recv()

    for copy in tok_copies:
        copy.wait()
    start_own(0)

    row = jnp.broadcast_to(seq_ref[...].astype(F32), (T, T))
    same = (row == row.T).astype(F32)
    tok_weight = T / (SEGS * jnp.sum(same, axis=1, keepdims=True))
    cot_copy.wait()
    for b in range(bd):
        cotb[c, g * bd + b] = (
            stage[:, b * B : (b + 1) * B].astype(F32) * tok_weight
        ).astype(BF16)

    for s in range(1, half_ring + 1):
        if s == half_ring:
            start_own(1)
        serve(0, s)
    core_arrivals(0)
    for copy in w_copies:
        copy.wait()

    def forward(h, _):
        wcat = jnp.concatenate([wv[0, h], wv[1, h]], axis=1)
        gain = unit_ref[pl.ds(h0 + h, 1), :]
        for r in range(CORES):
            x = jnp.concatenate([tokb[r, inb_ref[h0 + h, l]] for l in range(L)], axis=1)
            x_t[h, r] = x.T
            pre = jnp.dot(x, wcat, preferred_element_type=F32) * in_scale
            gate, up = pre[:, :B], pre[:, B:]
            sig = 1.0 / (1.0 + jnp.exp(-gate))
            silu = gate * sig
            hid_t[h, r] = (silu * up * gain).astype(BF16).T
            fac[h, r, :, :B] = gain * up * (sig * (1.0 + gate * (1.0 - sig))) * out_scale
            fac[h, r, :, B:] = gain * silu * out_scale
        return 0

    for s in range(1, half_ring + 1):
        serve(1, s)
        lo, hi = (s - 1) * hh // half_ring, s * hh // half_ring
        if hi > lo:
            lax.fori_loop(lo, hi, forward, 0)
    core_arrivals(1)

    def backward(h, sums):
        wd = jnp.concatenate([wv[2, h, l * B : (l + 1) * B] for l in range(L)], axis=1)
        new = []
        for r in range(CORES):
            y = jnp.concatenate([cotb[r, outb_ref[h0 + h, l]] for l in range(L)], axis=1)
            dh = lax.dot_general(y, wd, (((1,), (1,)), ((), ())), preferred_element_type=F32)
            both = (jnp.concatenate([dh, dh], axis=1) * fac[h, r]).astype(BF16)
            down = jnp.dot(hid_t[h, r], y, preferred_element_type=F32)
            gdn[r, h] = down
            grad = jnp.dot(x_t[h, r], both, preferred_element_type=F32)
            ggu[r, h] = grad
            sq_in = jnp.sum((grad * grad).reshape(L * B // 8, 8, 2 * B), axis=0)
            sq_out = jnp.sum((down * down).reshape(B // 8, 8, L * B), axis=0)
            part = (sq_in[:, :B] + sq_in[:, B:]) * (in_scale * in_scale)
            for l in range(L):
                part = part + sq_out[:, l * B : (l + 1) * B] * (out_scale * out_scale)
            new.append(sums[r] + part)
        return tuple(new)

    zero = jnp.zeros((8, B), F32)
    sums = lax.fori_loop(0, hh, backward, (zero, zero))
    for r in range(CORES):
        sqb[lin, r] = sums[r]

    def sq_copy(n, mine):
        other = lax.rem(lin + n, group)
        ref = sqb.at[lin if mine else lax.rem(lin - n + group, group)]
        return pltpu.make_async_remote_copy(
            src_ref=ref,
            dst_ref=ref,
            send_sem=sq_send.at[n - 1],
            recv_sem=sq_recv.at[n - 1],
            device_id=(p * CORES + lax.rem(other, CORES), other // CORES),
            device_id_type=MESH,
        )

    def sq_start(n, _):
        sq_copy(n, True).start()
        return 0

    def sq_wait(n, _):
        sq_copy(n, False).wait_recv()
        return 0

    lax.fori_loop(1, group, sq_start, 0)
    lax.fori_loop(1, group, sq_wait, 0)
    steps = []
    for r in range(CORES):
        total = jnp.sum(sqb[:, r], axis=0)
        total = jnp.sum(jnp.sum(total, axis=1, keepdims=True), axis=0, keepdims=True)
        rms = jnp.sqrt(total / count_all + 1e-06)
        steps.append(-LEARN_RATE * jnp.minimum(1.0, MAX_RMS / rms))

    def x_copy(h, n, mine):
        ref = xb.at[p if mine else lax.rem(p - n + peers, peers), h]
        return pltpu.make_async_remote_copy(
            src_ref=ref,
            dst_ref=ref,
            send_sem=x_send.at[n - 1, h],
            recv_sem=x_recv.at[n - 1, h],
            device_id=(lax.rem(p + n, peers) * CORES + c, g),
            device_id_type=MESH,
        )

    def deltas(h, _):
        gu = ggu[0, h] * (steps[0] * in_scale) + ggu[1, h] * (steps[1] * in_scale)
        dn = gdn[0, h] * (steps[0] * out_scale) + gdn[1, h] * (steps[1] * out_scale)
        xb[p, h, 0] = gu[:, :B].astype(BF16)
        xb[p, h, 1] = gu[:, B:].astype(BF16)
        for l in range(L):
            xb[p, h, 2, l * B : (l + 1) * B] = dn[:, l * B : (l + 1) * B].astype(BF16)
        for n in range(1, peers):
            x_copy(h, n, True).start()
        return 0

    lax.fori_loop(0, hh, deltas, 0)

    outs = (og_hbm, ou_hbm, od_hbm)

    def out_copies(h, j):
        return (
            pltpu.make_async_copy(wv.at[j, h], outs[j].at[h0 + h], out_local.at[j, h]),
            pltpu.make_async_remote_copy(
                src_ref=wv.at[j, h],
                dst_ref=outs[j].at[h0 + h],
                send_sem=out_send.at[j, h],
                recv_sem=out_recv.at[j, h],
                device_id=sib,
                device_id_type=MESH,
            ),
        )

    def update(h, _):
        for n in range(1, peers):
            x_copy(h, n, False).wait_recv()
        for j in range(3):
            total = xb[0, h, j].astype(F32)
            for q in range(1, peers):
                total = total + xb[q, h, j].astype(F32)
            wv[j, h] = (wv[j, h].astype(F32) + total * (1.0 / R)).astype(BF16)
            for copy in out_copies(h, j):
                copy.start()
        return 0

    lax.fori_loop(0, hh, update, 0)

    for k in range(2):
        for sub in range(2):
            core_copy(0, 0, k, sub, True).wait_send()
            for s in range(1, half_ring + 1):
                for way in range(2):
                    if in_step(way, s, sub):
                        ring_copy(way, s, k, sub).wait_send()
                        core_copy(way, s, k, sub, True).wait_send()

    def sq_sent(n, _):
        sq_copy(n, True).wait_send()
        return 0

    lax.fori_loop(1, group, sq_sent, 0)

    def finish(h, _):
        for n in range(1, peers):
            x_copy(h, n, True).wait_send()
        for j in range(3):
            local, remote = out_copies(h, j)
            local.wait()
            remote.wait_send()
            theirs = outs[j].at[(1 - c) * hh + h]
            pltpu.make_async_remote_copy(
                src_ref=theirs,
                dst_ref=theirs,
                send_sem=out_send.at[j, h],
                recv_sem=out_recv.at[j, h],
                device_id=sib,
                device_id_type=MESH,
            ).wait_recv()
        return 0

    lax.fori_loop(0, hh, finish, 0)


def per_device(
    G, R, tokens, cotangent, seq_ids, in_blocks, out_blocks, unit_scale, gate_w, up_w, down_w
):
    T, width = tokens.shape
    hb, L, B, _ = gate_w.shape
    bd = width // B
    nb, ff, d_model = bd * G, hb * G * B, width * G
    hh, peers, half = hb // CORES, R // CORES, G // 2
    cfg = dict(
        G=G,
        R=R,
        T=T,
        bd=bd,
        hb=hb,
        L=L,
        B=B,
        in_scale=float((L * B) ** -0.5),
        out_scale=float((L * B * (ff // d_model)) ** -0.5),
        count_all=float(3 * hb * G * L * B * B),
    )
    flat = lambda w: w.reshape(hb, L * B, B)
    any_spec = pl.BlockSpec(memory_space=pl.ANY)
    vmem = pl.BlockSpec(memory_space=pltpu.VMEM)
    smem = pl.BlockSpec(memory_space=pltpu.SMEM)
    dma = pltpu.SemaphoreType.DMA
    outs = pl.pallas_call(
        functools.partial(kernel, cfg),
        out_shape=[jax.ShapeDtypeStruct((hb, L * B, B), BF16)] * 3,
        in_specs=[any_spec, any_spec, vmem, smem, smem, vmem, any_spec, any_spec, any_spec],
        out_specs=[any_spec] * 3,
        scratch_shapes=[
            pltpu.VMEM((CORES, nb, T, B), BF16),
            pltpu.VMEM((CORES, nb, T, B), BF16),
            pltpu.VMEM((T, width), BF16),
            pltpu.VMEM((3, hh, L * B, B), BF16),
            pltpu.VMEM((hh, CORES, T, 2 * B), F32),
            pltpu.VMEM((hh, CORES, B, T), BF16),
            pltpu.VMEM((hh, CORES, L * B, T), BF16),
            pltpu.VMEM((CORES, hh, L * B, 2 * B), F32),
            pltpu.VMEM((CORES, hh, B, L * B), F32),
            pltpu.VMEM((peers, hh, 3, L * B, B), BF16),
            pltpu.VMEM((G * CORES, CORES, 8, B), F32),
            dma((bd,)),
            dma,
            dma((3,)),
            dma((2, half, 2, 2)),
            dma((2, half, 2, 2)),
            dma((2, 2)),
            dma((2, 2)),
            dma((2, half, 2, 2)),
            dma((2, half, 2, 2)),
            dma((G * CORES - 1,)),
            dma((G * CORES - 1,)),
            dma((peers - 1, hh)),
            dma((peers - 1, hh)),
            dma((3, hh)),
            dma((3, hh)),
            dma((3, hh)),
        ],
        compiler_params=pltpu.CompilerParams(
            collective_id=0, has_side_effects=True, vmem_limit_bytes=60 * 1024 * 1024
        ),
    )(
        tokens,
        cotangent,
        seq_ids,
        in_blocks,
        out_blocks,
        unit_scale.reshape(hb, B),
        flat(gate_w),
        flat(up_w),
        flat(down_w),
    )
    return tuple(o.reshape(hb, L, B, B) for o in outs)


def solution(mesh):
    return jax.shard_map(
        functools.partial(per_device, mesh.shape["hid"], mesh.shape["rep"]),
        mesh=mesh,
        in_specs=(
            P("rep", "hid"),
            P("rep", "hid"),
            P("rep", None),
            P("hid", None),
            P("hid", None),
            P("hid"),
            P("hid", None, None, None),
            P("hid", None, None, None),
            P("hid", None, None, None),
        ),
        out_specs=(
            P("hid", None, None, None),
            P("hid", None, None, None),
            P("hid", None, None, None),
        ),
        check_vma=False,
    )
```

```python
import functools

import jax
import jax.numpy as jnp
from jax import lax
from jax.experimental import pallas as pl
from jax.experimental.pallas import tpu as pltpu
from jax.sharding import PartitionSpec as P

MESH = pl.DeviceIdType.MESH
F32 = jnp.float32
BF16 = jnp.bfloat16
SEGS = 8
LEARN_RATE = 8.0
MAX_RMS = 0.1
CORES = 2


def kernel(
    cfg,
    tok_hbm,
    cot_hbm,
    seq_hbm,
    inb_hbm,
    outb_hbm,
    unit_hbm,
    wg_hbm,
    wu_hbm,
    wd_hbm,
    og,
    ou,
    od,
    tokb,
    cotb,
    stage,
    fac,
    hid_t,
    x_t,
    ggu,
    gdn,
    xb,
    sqb,
    seq_ref,
    unit_ref,
    inb_ref,
    outb_ref,
    small_sem,
    load_sem,
    stage_sem,
    w_sem,
    ring_send,
    ring_recv,
    own_send,
    own_recv,
    core_send,
    core_recv,
    sq_send,
    sq_recv,
    x_send,
    x_recv,
    out_send,
    out_recv,
):
    G, R, T, bd, hb, L, B = (cfg[k] for k in ("G", "R", "T", "bd", "hb", "L", "B"))
    in_scale, out_scale, count_all = cfg["in_scale"], cfg["out_scale"], cfg["count_all"]
    peers = R // CORES
    half_ring = G // 2
    depth = G // 2
    hh = hb // CORES
    sub_n = bd // 2
    group = G * CORES

    rep, g = lax.axis_index("rep"), lax.axis_index("hid")
    c, p = lax.rem(rep, CORES), rep // CORES
    lin = g * CORES + c
    sib = (p * CORES + (1 - c), g)
    gy, gz = lax.rem(g, 2), g // 2
    pos = gz + gy * (2 * depth - 1 - 2 * gz)

    def ring_at(q):
        q = lax.rem(q + 2 * G, G)
        y, z = q // depth, lax.rem(q, depth)
        return (z + y * (depth - 1 - 2 * z)) * 2 + y

    right, left = (rep, ring_at(pos + 1)), (rep, ring_at(pos - 1))
    h0 = c * hh
    bufs = (tokb, cotb)
    outs = (og, ou, od)

    w_copies = [
        pltpu.make_async_copy(src.at[pl.ds(h0, hh)], outs[j].at[pl.ds(h0, hh)], w_sem.at[j])
        for j, src in enumerate((wg_hbm, wu_hbm, wd_hbm))
    ]
    tok_copies = [
        pltpu.make_async_copy(
            tok_hbm.at[:, pl.ds(b * B, B)], tokb.at[c, g * bd + b], load_sem.at[b]
        )
        for b in range(bd)
    ]
    cot_copy = pltpu.make_async_copy(cot_hbm, stage, stage_sem)
    for copy in tok_copies:
        copy.start()
    cot_copy.start()
    small_copies = [
        pltpu.make_async_copy(src, dst, small_sem.at[n])
        for n, (src, dst) in enumerate(
            (
                (seq_hbm, seq_ref),
                (unit_hbm, unit_ref),
                (inb_hbm, inb_ref),
                (outb_hbm, outb_ref),
            )
        )
    ]
    for copy in small_copies:
        copy.start()
    for copy in w_copies:
        copy.start()

    barrier = pltpu.get_barrier_semaphore()

    def greet(n, _):
        other = lax.rem(lin + n, group)
        pl.semaphore_signal(
            barrier,
            inc=1,
            device_id=(p * CORES + lax.rem(other, CORES), other // CORES),
            device_id_type=MESH,
        )
        return 0

    lax.fori_loop(1, group, greet, 0)
    for n in range(1, peers):
        pl.semaphore_signal(
            barrier,
            inc=1,
            device_id=(lax.rem(p + n, peers) * CORES + c, g),
            device_id_type=MESH,
        )
    pl.semaphore_wait(barrier, group - 1 + peers - 1)

    def blocks_of(k, origin, sub):
        return bufs[k].at[c, pl.ds(origin * bd + sub * sub_n, sub_n)]

    def ring_copy(way, s, k, sub):
        origin = ring_at(pos - (s - 1)) if way == 0 else ring_at(pos + (s - 1))
        ref = blocks_of(k, origin, sub)
        return pltpu.make_async_remote_copy(
            src_ref=ref,
            dst_ref=ref,
            send_sem=ring_send.at[way, s - 1, k, sub],
            recv_sem=ring_recv.at[way, s - 1, k, sub],
            device_id=right if way == 0 else left,
            device_id_type=MESH,
        )

    def ring_arrival(way, s, k, sub):
        origin = ring_at(pos - s) if way == 0 else ring_at(pos + s)
        ref = blocks_of(k, origin, sub)
        return pltpu.make_async_remote_copy(
            src_ref=ref,
            dst_ref=ref,
            send_sem=ring_send.at[way, s - 1, k, sub],
            recv_sem=ring_recv.at[way, s - 1, k, sub],
            device_id=right if way == 0 else left,
            device_id_type=MESH,
        )

    def in_step(way, s, sub):
        return s < half_ring or (s == half_ring and way == sub)

    def core_copy(way, s, k, sub, mine):
        origin = g if s == 0 else (ring_at(pos - s) if way == 0 else ring_at(pos + s))
        who = c if mine else 1 - c
        ref = bufs[k].at[who, pl.ds(origin * bd + sub * sub_n, sub_n)]
        if s == 0:
            sems = own_send.at[k, sub], own_recv.at[k, sub]
        else:
            sems = core_send.at[way, s - 1, k, sub], core_recv.at[way, s - 1, k, sub]
        return pltpu.make_async_remote_copy(
            src_ref=ref,
            dst_ref=ref,
            send_sem=sems[0],
            recv_sem=sems[1],
            device_id=sib,
            device_id_type=MESH,
        )

    def start_own(k):
        for sub in range(2):
            for way in range(2):
                if in_step(way, 1, sub):
                    ring_copy(way, 1, k, sub).start()
        for sub in range(2):
            core_copy(0, 0, k, sub, True).start()

    def serve(k, s):
        for sub in range(2):
            for way in range(2):
                if not in_step(way, s, sub):
                    continue
                ring_arrival(way, s, k, sub).wait_recv()
                if in_step(way, s + 1, sub):
                    ring_copy(way, s + 1, k, sub).start()
                core_copy(way, s, k, sub, True).start()

    def core_arrivals(k):
        for sub in range(2):
            core_copy(0, 0, k, sub, False).wait_recv()
            for s in range(1, half_ring + 1):
                for way in range(2):
                    if in_step(way, s, sub):
                        core_copy(way, s, k, sub, False).wait_recv()

    for copy in tok_copies:
        copy.wait()
    start_own(0)

    for copy in small_copies:
        copy.wait()
    row = jnp.broadcast_to(seq_ref[...].astype(F32), (T, T))
    same = (row == row.T).astype(F32)
    tok_weight = T / (SEGS * jnp.sum(same, axis=1, keepdims=True))
    cot_copy.wait()
    for b in range(bd):
        cotb[c, g * bd + b] = (
            stage[:, b * B : (b + 1) * B].astype(F32) * tok_weight
        ).astype(BF16)

    for s in range(1, half_ring + 1):
        if s == max(1, half_ring - 1):
            start_own(1)
        serve(0, s)
    core_arrivals(0)
    for copy in w_copies:
        copy.wait()

    def forward(h, _):
        wcat = jnp.concatenate([og[h0 + h], ou[h0 + h]], axis=1)
        gain = unit_ref[pl.ds(h0 + h, 1), :]
        for r in range(CORES):
            x = jnp.concatenate([tokb[r, inb_ref[l, h0 + h]] for l in range(L)], axis=1)
            x_t[h, r] = x.T
            pre = jnp.dot(x, wcat, preferred_element_type=F32) * in_scale
            gate, up = pre[:, :B], pre[:, B:]
            sig = 1.0 / (1.0 + jnp.exp(-gate))
            silu = gate * sig
            hid_t[h, r] = (silu * up * gain).astype(BF16).T
            fac[h, r, :, :B] = gain * up * (sig * (1.0 + gate * (1.0 - sig))) * out_scale
            fac[h, r, :, B:] = gain * silu * out_scale
        return 0

    for s in range(1, half_ring + 1):
        serve(1, s)
        lo, hi = (s - 1) * hh // half_ring, s * hh // half_ring
        if hi > lo:
            lax.fori_loop(lo, hi, forward, 0)
    core_arrivals(1)

    def backward(h, sums):
        return backward_one(h * 2 + 1, backward_one(h * 2, sums)) if hh % 2 == 0 else backward_one(h, sums)

    def backward_one(h, sums):
        wd = jnp.concatenate([od[h0 + h, l * B : (l + 1) * B] for l in range(L)], axis=1)
        new = []
        for r in range(CORES):
            y = jnp.concatenate([cotb[r, outb_ref[l, h0 + h]] for l in range(L)], axis=1)
            dh = lax.dot_general(y, wd, (((1,), (1,)), ((), ())), preferred_element_type=F32)
            both = (jnp.concatenate([dh, dh], axis=1) * fac[h, r]).astype(BF16)
            down = jnp.dot(hid_t[h, r], y, preferred_element_type=F32)
            gdn[r, h] = down
            grad = jnp.dot(x_t[h, r], both, preferred_element_type=F32)
            ggu[r, h] = grad
            sq_in = jnp.sum((grad * grad).reshape(L * B // 8, 8, 2 * B), axis=0)
            sq_out = jnp.sum((down * down).reshape(B // 8, 8, L * B), axis=0)
            part = (sq_in[:, :B] + sq_in[:, B:]) * (in_scale * in_scale)
            for l in range(L):
                part = part + sq_out[:, l * B : (l + 1) * B] * (out_scale * out_scale)
            new.append(sums[r] + part)
        return tuple(new)

    zero = jnp.zeros((8, B), F32)
    sums = lax.fori_loop(0, hh // 2 if hh % 2 == 0 else hh, backward, (zero, zero))
    for r in range(CORES):
        sqb[lin, r] = sums[r]

    def sq_copy(n, mine):
        other = lax.rem(lin + n, group)
        ref = sqb.at[lin if mine else lax.rem(lin - n + group, group)]
        return pltpu.make_async_remote_copy(
            src_ref=ref,
            dst_ref=ref,
            send_sem=sq_send.at[n - 1],
            recv_sem=sq_recv.at[n - 1],
            device_id=(p * CORES + lax.rem(other, CORES), other // CORES),
            device_id_type=MESH,
        )

    def sq_start(n, _):
        sq_copy(n, True).start()
        return 0

    def sq_wait(n, _):
        sq_copy(n, False).wait_recv()
        return 0

    lax.fori_loop(1, group, sq_start, 0)
    lax.fori_loop(1, group, sq_wait, 0)
    steps = []
    for r in range(CORES):
        total = jnp.sum(sqb[:, r], axis=0)
        total = jnp.sum(jnp.sum(total, axis=1, keepdims=True), axis=0, keepdims=True)
        rms = jnp.sqrt(total / count_all + 1e-06)
        steps.append(-LEARN_RATE * jnp.minimum(1.0, MAX_RMS / rms))

    def x_copy(h, j, n, mine):
        ref = xb.at[p if mine else lax.rem(p - n + peers, peers), h, j]
        return pltpu.make_async_remote_copy(
            src_ref=ref,
            dst_ref=ref,
            send_sem=x_send.at[n - 1, h, j],
            recv_sem=x_recv.at[n - 1, h, j],
            device_id=(lax.rem(p + n, peers) * CORES + c, g),
            device_id_type=MESH,
        )

    def deltas(h, _):
        gu = ggu[0, h] * (steps[0] * in_scale) + ggu[1, h] * (steps[1] * in_scale)
        xb[p, h, 0] = gu[:, :B].astype(BF16)
        xb[p, h, 1] = gu[:, B:].astype(BF16)
        for n in range(1, peers):
            x_copy(h, 0, n, True).start()
            x_copy(h, 1, n, True).start()
        dn = gdn[0, h] * (steps[0] * out_scale) + gdn[1, h] * (steps[1] * out_scale)
        for l in range(L):
            xb[p, h, 2, l * B : (l + 1) * B] = dn[:, l * B : (l + 1) * B].astype(BF16)
        for n in range(1, peers):
            x_copy(h, 2, n, True).start()
        return 0

    lax.fori_loop(0, hh, deltas, 0)

    def out_copy(h, j, mine):
        ref = outs[j].at[(h0 if mine else (1 - c) * hh) + h]
        return pltpu.make_async_remote_copy(
            src_ref=ref,
            dst_ref=ref,
            send_sem=out_send.at[j, h],
            recv_sem=out_recv.at[j, h],
            device_id=sib,
            device_id_type=MESH,
        )

    def update(h, _):
        for j in range(3):
            for n in range(1, peers):
                x_copy(h, j, n, False).wait_recv()
            total = xb[0, h, j].astype(F32)
            for q in range(1, peers):
                total = total + xb[q, h, j].astype(F32)
            new = outs[j][h0 + h].astype(F32) + total * (1.0 / R)
            outs[j][h0 + h] = new.astype(BF16)
            out_copy(h, j, True).start()
        return 0

    lax.fori_loop(0, hh, update, 0)

    for k in range(2):
        for sub in range(2):
            core_copy(0, 0, k, sub, True).wait_send()
            for s in range(1, half_ring + 1):
                for way in range(2):
                    if in_step(way, s, sub):
                        ring_copy(way, s, k, sub).wait_send()
                        core_copy(way, s, k, sub, True).wait_send()

    def sq_sent(n, _):
        sq_copy(n, True).wait_send()
        return 0

    lax.fori_loop(1, group, sq_sent, 0)

    def finish(h, _):
        for n in range(1, peers):
            for j in range(3):
                x_copy(h, j, n, True).wait_send()
        for j in range(3):
            out_copy(h, j, True).wait_send()
            out_copy(h, j, False).wait_recv()
        return 0

    lax.fori_loop(0, hh, finish, 0)


def per_device(
    G, R, tokens, cotangent, seq_ids, in_blocks, out_blocks, unit_scale, gate_w, up_w, down_w
):
    T, width = tokens.shape
    hb, L, B, _ = gate_w.shape
    bd = width // B
    nb, ff, d_model = bd * G, hb * G * B, width * G
    hh, peers, half = hb // CORES, R // CORES, G // 2
    cfg = dict(
        G=G,
        R=R,
        T=T,
        bd=bd,
        hb=hb,
        L=L,
        B=B,
        in_scale=float((L * B) ** -0.5),
        out_scale=float((L * B * (ff // d_model)) ** -0.5),
        count_all=float(3 * hb * G * L * B * B),
    )
    flat = lambda w: w.reshape(hb, L * B, B)
    any_spec = pl.BlockSpec(memory_space=pl.ANY)
    dma = pltpu.SemaphoreType.DMA
    outs = pl.pallas_call(
        functools.partial(kernel, cfg),
        out_shape=[pltpu.VMEM((hb, L * B, B), BF16)] * 3,
        in_specs=[any_spec] * 9,
        out_specs=[pl.BlockSpec(memory_space=pltpu.VMEM)] * 3,
        scratch_shapes=[
            pltpu.VMEM((CORES, nb, T, B), BF16),
            pltpu.VMEM((CORES, nb, T, B), BF16),
            pltpu.VMEM((T, width), BF16),
            pltpu.VMEM((hh, CORES, T, 2 * B), F32),
            pltpu.VMEM((hh, CORES, B, T), BF16),
            pltpu.VMEM((hh, CORES, L * B, T), BF16),
            pltpu.VMEM((CORES, hh, L * B, 2 * B), F32),
            pltpu.VMEM((CORES, hh, B, L * B), F32),
            pltpu.VMEM((peers, hh, 3, L * B, B), BF16),
            pltpu.VMEM((G * CORES, CORES, 8, B), F32),
            pltpu.VMEM((1, T), jnp.int32),
            pltpu.VMEM((hb, B), F32),
            pltpu.SMEM((L, hb), jnp.int32),
            pltpu.SMEM((L, hb), jnp.int32),
            dma((4,)),
            dma((bd,)),
            dma,
            dma((3,)),
            dma((2, half, 2, 2)),
            dma((2, half, 2, 2)),
            dma((2, 2)),
            dma((2, 2)),
            dma((2, half, 2, 2)),
            dma((2, half, 2, 2)),
            dma((G * CORES - 1,)),
            dma((G * CORES - 1,)),
            dma((peers - 1, hh, 3)),
            dma((peers - 1, hh, 3)),
            dma((3, hh)),
            dma((3, hh)),
        ],
        compiler_params=pltpu.CompilerParams(
            collective_id=0, has_side_effects=True, vmem_limit_bytes=56 * 1024 * 1024
        ),
    )(
        tokens,
        cotangent,
        seq_ids,
        in_blocks.T,
        out_blocks.T,
        unit_scale.reshape(hb, B),
        flat(gate_w),
        flat(up_w),
        flat(down_w),
    )
    return tuple(o.reshape(hb, L, B, B) for o in outs)


def solution(mesh):
    return jax.shard_map(
        functools.partial(per_device, mesh.shape["hid"], mesh.shape["rep"]),
        mesh=mesh,
        in_specs=(
            P("rep", "hid"),
            P("rep", "hid"),
            P("rep", None),
            P("hid", None),
            P("hid", None),
            P("hid"),
            P("hid", None, None, None),
            P("hid", None, None, None),
            P("hid", None, None, None),
        ),
        out_specs=(
            P("hid", None, None, None),
            P("hid", None, None, None),
            P("hid", None, None, None),
        ),
        check_vma=False,
    )
```

```python
import functools

import jax
import jax.numpy as jnp
from jax import lax
from jax.experimental import pallas as pl
from jax.experimental.pallas import tpu as pltpu
from jax.sharding import PartitionSpec as P

MESH = pl.DeviceIdType.MESH
F32 = jnp.float32
BF16 = jnp.bfloat16
SEGS = 8
LEARN_RATE = 8.0
MAX_RMS = 0.1
CORES = 2


def kernel(
    cfg,
    tok_hbm,
    cot_hbm,
    seq_hbm,
    inb_hbm,
    outb_hbm,
    unit_hbm,
    wg_hbm,
    wu_hbm,
    wd_hbm,
    og,
    ou,
    od,
    tokb,
    cotb,
    stage,
    fac,
    hid_t,
    x_t,
    ggu,
    gdn,
    xb,
    sqb,
    eb,
    stb,
    early_send,
    early_recv,
    seq_ref,
    unit_ref,
    inb_ref,
    outb_ref,
    small_sem,
    load_sem,
    stage_sem,
    w_sem,
    ring_send,
    ring_recv,
    own_send,
    own_recv,
    core_send,
    core_recv,
    sq_send,
    sq_recv,
    x_send,
    x_recv,
    out_send,
    out_recv,
):
    G, R, T, bd, hb, L, B = (cfg[k] for k in ("G", "R", "T", "bd", "hb", "L", "B"))
    in_scale, out_scale, count_all = cfg["in_scale"], cfg["out_scale"], cfg["count_all"]
    peers = R // CORES
    half_ring = G // 2
    depth = G // 2
    hh = hb // CORES
    subs = cfg["subs"]
    sub_n = bd // subs
    group = G * CORES

    rep, g = lax.axis_index("rep"), lax.axis_index("hid")
    c, p = lax.rem(rep, CORES), rep // CORES
    lin = g * CORES + c
    sib = (p * CORES + (1 - c), g)
    gy, gz = lax.rem(g, 2), g // 2
    pos = gz + gy * (2 * depth - 1 - 2 * gz)

    def ring_at(q):
        q = lax.rem(q + 2 * G, G)
        y, z = q // depth, lax.rem(q, depth)
        return (z + y * (depth - 1 - 2 * z)) * 2 + y

    right, left = (rep, ring_at(pos + 1)), (rep, ring_at(pos - 1))
    h0 = c * hh
    bufs = (tokb, cotb)
    outs = (og, ou, od)

    w_copies = [
        pltpu.make_async_copy(src.at[pl.ds(h0, hh)], outs[j].at[pl.ds(h0, hh)], w_sem.at[j])
        for j, src in enumerate((wg_hbm, wu_hbm, wd_hbm))
    ]
    tok_copies = [
        pltpu.make_async_copy(
            tok_hbm.at[:, pl.ds(b * B, B)], tokb.at[c, g * bd + b], load_sem.at[b]
        )
        for b in range(bd)
    ]
    cot_copy = pltpu.make_async_copy(cot_hbm, stage, stage_sem)
    for copy in tok_copies:
        copy.start()
    cot_copy.start()
    small_copies = [
        pltpu.make_async_copy(src, dst, small_sem.at[n])
        for n, (src, dst) in enumerate(
            (
                (seq_hbm, seq_ref),
                (unit_hbm, unit_ref),
                (inb_hbm, inb_ref),
                (outb_hbm, outb_ref),
            )
        )
    ]
    for copy in small_copies:
        copy.start()
    for copy in w_copies:
        copy.start()

    barrier = pltpu.get_barrier_semaphore()

    def greet(n, _):
        other = lax.rem(lin + n, group)
        pl.semaphore_signal(
            barrier,
            inc=1,
            device_id=(p * CORES + lax.rem(other, CORES), other // CORES),
            device_id_type=MESH,
        )
        return 0

    lax.fori_loop(1, group, greet, 0)
    for n in range(1, peers):
        pl.semaphore_signal(
            barrier,
            inc=1,
            device_id=(lax.rem(p + n, peers) * CORES + c, g),
            device_id_type=MESH,
        )
    pl.semaphore_wait(barrier, group - 1 + peers - 1)

    def blocks_of(k, origin, sub):
        return bufs[k].at[c, pl.ds(origin * bd + sub * sub_n, sub_n)]

    def ring_copy(way, s, k, sub):
        origin = ring_at(pos - (s - 1)) if way == 0 else ring_at(pos + (s - 1))
        ref = blocks_of(k, origin, sub)
        return pltpu.make_async_remote_copy(
            src_ref=ref,
            dst_ref=ref,
            send_sem=ring_send.at[way, s - 1, k, sub],
            recv_sem=ring_recv.at[way, s - 1, k, sub],
            device_id=right if way == 0 else left,
            device_id_type=MESH,
        )

    def ring_arrival(way, s, k, sub):
        origin = ring_at(pos - s) if way == 0 else ring_at(pos + s)
        ref = blocks_of(k, origin, sub)
        return pltpu.make_async_remote_copy(
            src_ref=ref,
            dst_ref=ref,
            send_sem=ring_send.at[way, s - 1, k, sub],
            recv_sem=ring_recv.at[way, s - 1, k, sub],
            device_id=right if way == 0 else left,
            device_id_type=MESH,
        )

    def in_step(way, s, sub):
        return s < half_ring or (s == half_ring and way == sub // (subs // 2))

    def core_copy(way, s, k, sub, mine):
        origin = g if s == 0 else (ring_at(pos - s) if way == 0 else ring_at(pos + s))
        who = c if mine else 1 - c
        ref = bufs[k].at[who, pl.ds(origin * bd + sub * sub_n, sub_n)]
        if s == 0:
            sems = own_send.at[k, sub], own_recv.at[k, sub]
        else:
            sems = core_send.at[way, s - 1, k, sub], core_recv.at[way, s - 1, k, sub]
        return pltpu.make_async_remote_copy(
            src_ref=ref,
            dst_ref=ref,
            send_sem=sems[0],
            recv_sem=sems[1],
            device_id=sib,
            device_id_type=MESH,
        )

    def start_own(k):
        for sub in range(subs):
            for way in range(2):
                if in_step(way, 1, sub):
                    ring_copy(way, 1, k, sub).start()
        for sub in range(subs):
            core_copy(0, 0, k, sub, True).start()

    def serve(k, s):
        for sub in range(subs):
            for way in range(2):
                if not in_step(way, s, sub):
                    continue
                ring_arrival(way, s, k, sub).wait_recv()
                if in_step(way, s + 1, sub):
                    ring_copy(way, s + 1, k, sub).start()
                core_copy(way, s, k, sub, True).start()

    def core_arrivals(k):
        for sub in range(subs):
            core_copy(0, 0, k, sub, False).wait_recv()
            for s in range(1, half_ring + 1):
                for way in range(2):
                    if in_step(way, s, sub):
                        core_copy(way, s, k, sub, False).wait_recv()

    for copy in tok_copies:
        copy.wait()
    start_own(0)

    for copy in small_copies:
        copy.wait()
    row = jnp.broadcast_to(seq_ref[...].astype(F32), (T, T))
    same = (row == row.T).astype(F32)
    tok_weight = T / (SEGS * jnp.sum(same, axis=1, keepdims=True))
    cot_copy.wait()
    for b in range(bd):
        cotb[c, g * bd + b] = (
            stage[:, b * B : (b + 1) * B].astype(F32) * tok_weight
        ).astype(BF16)

    for s in range(1, half_ring + 1):
        if s == max(1, half_ring - 1):
            start_own(1)
        serve(0, s)
    core_arrivals(0)
    for copy in w_copies:
        copy.wait()

    def forward(h, _):
        wcat = jnp.concatenate([og[h0 + h], ou[h0 + h]], axis=1)
        gain = unit_ref[pl.ds(h0 + h, 1), :]
        for r in range(CORES):
            x = jnp.concatenate([tokb[r, inb_ref[l, h0 + h]] for l in range(L)], axis=1)
            x_t[h, r] = x.T
            pre = jnp.dot(x, wcat, preferred_element_type=F32) * in_scale
            gate, up = pre[:, :B], pre[:, B:]
            sig = 1.0 / (1.0 + jnp.exp(-gate))
            silu = gate * sig
            hid_t[h, r] = (silu * up * gain).astype(BF16).T
            fac[h, r, :, :B] = gain * up * (sig * (1.0 + gate * (1.0 - sig))) * out_scale
            fac[h, r, :, B:] = gain * silu * out_scale
        return 0

    for s in range(1, half_ring + 1):
        serve(1, s)
        lo, hi = (s - 1) * hh // half_ring, s * hh // half_ring
        if hi > lo:
            lax.fori_loop(lo, hi, forward, 0)
    core_arrivals(1)

    def backward(h, sums):
        return backward_one(h * 2 + 1, backward_one(h * 2, sums)) if hh % 2 == 0 else backward_one(h, sums)

    def backward_one(h, sums):
        wd = jnp.concatenate([od[h0 + h, l * B : (l + 1) * B] for l in range(L)], axis=1)
        new = []
        for r in range(CORES):
            y = jnp.concatenate([cotb[r, outb_ref[l, h0 + h]] for l in range(L)], axis=1)
            dh = lax.dot_general(y, wd, (((1,), (1,)), ((), ())), preferred_element_type=F32)
            both = (jnp.concatenate([dh, dh], axis=1) * fac[h, r]).astype(BF16)
            down = jnp.dot(hid_t[h, r], y, preferred_element_type=F32)
            gdn[r, h] = down
            grad = jnp.dot(x_t[h, r], both, preferred_element_type=F32)
            ggu[r, h] = grad
            sq_in = jnp.sum((grad * grad).reshape(L * B // 8, 8, 2 * B), axis=0)
            sq_out = jnp.sum((down * down).reshape(B // 8, 8, L * B), axis=0)
            part = (sq_in[:, :B] + sq_in[:, B:]) * (in_scale * in_scale)
            for l in range(L):
                part = part + sq_out[:, l * B : (l + 1) * B] * (out_scale * out_scale)
            new.append(sums[r] + part)
        return tuple(new)

    zero = jnp.zeros((8, B), F32)
    sums = backward_one(0, (zero, zero))

    def early_copy(which, n, mine):
        ref = (eb, stb)[which].at[p if mine else lax.rem(p - n + peers, peers)]
        return pltpu.make_async_remote_copy(
            src_ref=ref,
            dst_ref=ref,
            send_sem=early_send.at[which, n - 1],
            recv_sem=early_recv.at[which, n - 1],
            device_id=(lax.rem(p + n, peers) * CORES + c, g),
            device_id_type=MESH,
        )

    for r in range(CORES):
        eb[p, r] = ggu[r, 0, :, :B].astype(BF16)
    for n in range(1, peers):
        early_copy(0, n, True).start()
    if hh % 2 == 0:
        sums = backward_one(1, sums)
    sums = lax.fori_loop(1, hh // 2 if hh % 2 == 0 else hh, backward, sums)
    for r in range(CORES):
        sqb[lin, r] = sums[r]

    def sq_copy(n, mine):
        other = lax.rem(lin + n, group)
        ref = sqb.at[lin if mine else lax.rem(lin - n + group, group)]
        return pltpu.make_async_remote_copy(
            src_ref=ref,
            dst_ref=ref,
            send_sem=sq_send.at[n - 1],
            recv_sem=sq_recv.at[n - 1],
            device_id=(p * CORES + lax.rem(other, CORES), other // CORES),
            device_id_type=MESH,
        )

    def sq_start(n, _):
        sq_copy(n, True).start()
        return 0

    def sq_wait(n, _):
        sq_copy(n, False).wait_recv()
        return 0

    lax.fori_loop(1, group, sq_start, 0)
    lax.fori_loop(1, group, sq_wait, 0)
    steps = []
    for r in range(CORES):
        total = jnp.sum(sqb[:, r], axis=0)
        total = jnp.sum(jnp.sum(total, axis=1, keepdims=True), axis=0, keepdims=True)
        rms = jnp.sqrt(total / count_all + 1e-06)
        steps.append(-LEARN_RATE * jnp.minimum(1.0, MAX_RMS / rms))

    for r in range(CORES):
        stb[p, r] = jnp.broadcast_to(steps[r] * in_scale, (8, B))
    for n in range(1, peers):
        early_copy(1, n, True).start()

    def x_copy(h, j, n, mine):
        ref = xb.at[p if mine else lax.rem(p - n + peers, peers), h, j]
        return pltpu.make_async_remote_copy(
            src_ref=ref,
            dst_ref=ref,
            send_sem=x_send.at[n - 1, h, j],
            recv_sem=x_recv.at[n - 1, h, j],
            device_id=(lax.rem(p + n, peers) * CORES + c, g),
            device_id_type=MESH,
        )

    def deltas(h, first):
        gu = ggu[0, h] * (steps[0] * in_scale) + ggu[1, h] * (steps[1] * in_scale)
        for j in range(1 if first else 0, 2):
            xb[p, h, j] = gu[:, j * B : (j + 1) * B].astype(BF16)
            for n in range(1, peers):
                x_copy(h, j, n, True).start()
        dn = gdn[0, h] * (steps[0] * out_scale) + gdn[1, h] * (steps[1] * out_scale)
        for l in range(L):
            xb[p, h, 2, l * B : (l + 1) * B] = dn[:, l * B : (l + 1) * B].astype(BF16)
        for n in range(1, peers):
            x_copy(h, 2, n, True).start()

    def deltas_step(h, _):
        deltas(h, False)
        return 0

    deltas(0, True)
    lax.fori_loop(1, hh, deltas_step, 0)

    def out_copy(h, j, mine):
        ref = outs[j].at[(h0 if mine else (1 - c) * hh) + h]
        return pltpu.make_async_remote_copy(
            src_ref=ref,
            dst_ref=ref,
            send_sem=out_send.at[j, h],
            recv_sem=out_recv.at[j, h],
            device_id=sib,
            device_id_type=MESH,
        )

    def update(h, first):
        for j in range(3):
            if first and j == 0:
                for n in range(1, peers):
                    early_copy(0, n, False).wait_recv()
                    early_copy(1, n, False).wait_recv()
                total = jnp.zeros((L * B, B), F32)
                for q in range(peers):
                    for r in range(CORES):
                        total = total + stb[q, r, 0:1] * eb[q, r].astype(F32)
            else:
                for n in range(1, peers):
                    x_copy(h, j, n, False).wait_recv()
                total = xb[0, h, j].astype(F32)
                for q in range(1, peers):
                    total = total + xb[q, h, j].astype(F32)
            new = outs[j][h0 + h].astype(F32) + total * (1.0 / R)
            outs[j][h0 + h] = new.astype(BF16)
            out_copy(h, j, True).start()

    def update_step(h, _):
        update(h, False)
        return 0

    update(0, True)
    lax.fori_loop(1, hh, update_step, 0)

    for k in range(2):
        for sub in range(subs):
            core_copy(0, 0, k, sub, True).wait_send()
            for s in range(1, half_ring + 1):
                for way in range(2):
                    if in_step(way, s, sub):
                        ring_copy(way, s, k, sub).wait_send()
                        core_copy(way, s, k, sub, True).wait_send()

    def sq_sent(n, _):
        sq_copy(n, True).wait_send()
        return 0

    lax.fori_loop(1, group, sq_sent, 0)

    def finish(h, first):
        for j in range(3):
            for n in range(1, peers):
                if first and j == 0:
                    early_copy(0, n, True).wait_send()
                    early_copy(1, n, True).wait_send()
                else:
                    x_copy(h, j, n, True).wait_send()
            out_copy(h, j, True).wait_send()
            out_copy(h, j, False).wait_recv()

    def finish_step(h, _):
        finish(h, False)
        return 0

    finish(0, True)
    lax.fori_loop(1, hh, finish_step, 0)


def per_device(
    G, R, tokens, cotangent, seq_ids, in_blocks, out_blocks, unit_scale, gate_w, up_w, down_w
):
    T, width = tokens.shape
    hb, L, B, _ = gate_w.shape
    bd = width // B
    nb, ff, d_model = bd * G, hb * G * B, width * G
    hh, peers, half = hb // CORES, R // CORES, G // 2
    subs = 4 if bd % 4 == 0 else 2
    cfg = dict(
        G=G,
        R=R,
        T=T,
        bd=bd,
        hb=hb,
        subs=subs,
        L=L,
        B=B,
        in_scale=float((L * B) ** -0.5),
        out_scale=float((L * B * (ff // d_model)) ** -0.5),
        count_all=float(3 * hb * G * L * B * B),
    )
    flat = lambda w: w.reshape(hb, L * B, B)
    any_spec = pl.BlockSpec(memory_space=pl.ANY)
    dma = pltpu.SemaphoreType.DMA
    outs = pl.pallas_call(
        functools.partial(kernel, cfg),
        out_shape=[pltpu.VMEM((hb, L * B, B), BF16)] * 3,
        in_specs=[any_spec] * 9,
        out_specs=[pl.BlockSpec(memory_space=pltpu.VMEM)] * 3,
        scratch_shapes=[
            pltpu.VMEM((CORES, nb, T, B), BF16),
            pltpu.VMEM((CORES, nb, T, B), BF16),
            pltpu.VMEM((T, width), BF16),
            pltpu.VMEM((hh, CORES, T, 2 * B), F32),
            pltpu.VMEM((hh, CORES, B, T), BF16),
            pltpu.VMEM((hh, CORES, L * B, T), BF16),
            pltpu.VMEM((CORES, hh, L * B, 2 * B), F32),
            pltpu.VMEM((CORES, hh, B, L * B), F32),
            pltpu.VMEM((peers, hh, 3, L * B, B), BF16),
            pltpu.VMEM((G * CORES, CORES, 8, B), F32),
            pltpu.VMEM((peers, CORES, L * B, B), BF16),
            pltpu.VMEM((peers, CORES, 8, B), F32),
            dma((2, peers - 1)),
            dma((2, peers - 1)),
            pltpu.VMEM((1, T), jnp.int32),
            pltpu.VMEM((hb, B), F32),
            pltpu.SMEM((L, hb), jnp.int32),
            pltpu.SMEM((L, hb), jnp.int32),
            dma((4,)),
            dma((bd,)),
            dma,
            dma((3,)),
            dma((2, half, 2, subs)),
            dma((2, half, 2, subs)),
            dma((2, subs)),
            dma((2, subs)),
            dma((2, half, 2, subs)),
            dma((2, half, 2, subs)),
            dma((G * CORES - 1,)),
            dma((G * CORES - 1,)),
            dma((peers - 1, hh, 3)),
            dma((peers - 1, hh, 3)),
            dma((3, hh)),
            dma((3, hh)),
        ],
        compiler_params=pltpu.CompilerParams(
            collective_id=0, has_side_effects=True, vmem_limit_bytes=56 * 1024 * 1024
        ),
    )(
        tokens,
        cotangent,
        seq_ids,
        in_blocks.T,
        out_blocks.T,
        unit_scale.reshape(hb, B),
        flat(gate_w),
        flat(up_w),
        flat(down_w),
    )
    return tuple(o.reshape(hb, L, B, B) for o in outs)


def solution(mesh):
    return jax.shard_map(
        functools.partial(per_device, mesh.shape["hid"], mesh.shape["rep"]),
        mesh=mesh,
        in_specs=(
            P("rep", "hid"),
            P("rep", "hid"),
            P("rep", None),
            P("hid", None),
            P("hid", None),
            P("hid"),
            P("hid", None, None, None),
            P("hid", None, None, None),
            P("hid", None, None, None),
        ),
        out_specs=(
            P("hid", None, None, None),
            P("hid", None, None, None),
            P("hid", None, None, None),
        ),
        check_vma=False,
    )
```

```python
import functools

import jax
import jax.numpy as jnp
from jax import lax
from jax.experimental import pallas as pl
from jax.experimental.pallas import tpu as pltpu
from jax.sharding import PartitionSpec as P

MESH = pl.DeviceIdType.MESH
F32 = jnp.float32
BF16 = jnp.bfloat16
SEGS = 8
LEARN_RATE = 8.0
MAX_RMS = 0.1
CORES = 2


def kernel(
    cfg,
    tok_hbm,
    cot_hbm,
    seq_hbm,
    inb_hbm,
    outb_hbm,
    unit_hbm,
    wg_hbm,
    wu_hbm,
    wd_hbm,
    og,
    ou,
    od,
    tokb,
    cotb,
    stage,
    fac,
    hid_t,
    x_t,
    ggu,
    gdn,
    xb,
    sqb,
    eb,
    stb,
    early_send,
    early_recv,
    seq_ref,
    unit_ref,
    inb_ref,
    outb_ref,
    small_sem,
    load_sem,
    stage_sem,
    w_sem,
    ring_send,
    ring_recv,
    own_send,
    own_recv,
    core_send,
    core_recv,
    sq_send,
    sq_recv,
    x_send,
    x_recv,
    out_send,
    out_recv,
):
    G, R, T, bd, hb, L, B = (cfg[k] for k in ("G", "R", "T", "bd", "hb", "L", "B"))
    in_scale, out_scale, count_all = cfg["in_scale"], cfg["out_scale"], cfg["count_all"]
    peers = R // CORES
    half_ring = G // 2
    depth = G // 2
    hh = hb // CORES
    subs = cfg["subs"]
    sub_n = bd // subs
    group = G * CORES

    rep, g = lax.axis_index("rep"), lax.axis_index("hid")
    c, p = lax.rem(rep, CORES), rep // CORES
    lin = g * CORES + c
    sib = (p * CORES + (1 - c), g)
    gy, gz = lax.rem(g, 2), g // 2
    pos = gz + gy * (2 * depth - 1 - 2 * gz)

    def ring_at(q):
        q = lax.rem(q + 2 * G, G)
        y, z = q // depth, lax.rem(q, depth)
        return (z + y * (depth - 1 - 2 * z)) * 2 + y

    right, left = (rep, ring_at(pos + 1)), (rep, ring_at(pos - 1))
    h0 = c * hh
    bufs = (tokb, cotb)
    outs = (og, ou, od)

    w_copies = [
        pltpu.make_async_copy(src.at[pl.ds(h0, hh)], outs[j].at[pl.ds(h0, hh)], w_sem.at[j])
        for j, src in enumerate((wg_hbm, wu_hbm, wd_hbm))
    ]
    tok_copies = [
        pltpu.make_async_copy(
            tok_hbm.at[:, pl.ds(b * B, B)], tokb.at[c, g * bd + b], load_sem.at[b]
        )
        for b in range(bd)
    ]
    cot_copy = pltpu.make_async_copy(cot_hbm, stage, stage_sem)
    for copy in tok_copies:
        copy.start()
    cot_copy.start()
    small_copies = [
        pltpu.make_async_copy(src, dst, small_sem.at[n])
        for n, (src, dst) in enumerate(
            (
                (seq_hbm, seq_ref),
                (unit_hbm, unit_ref),
                (inb_hbm, inb_ref),
                (outb_hbm, outb_ref),
            )
        )
    ]
    for copy in small_copies:
        copy.start()
    for copy in w_copies:
        copy.start()

    barrier = pltpu.get_barrier_semaphore()

    def greet(n, _):
        other = lax.rem(lin + n, group)
        pl.semaphore_signal(
            barrier,
            inc=1,
            device_id=(p * CORES + lax.rem(other, CORES), other // CORES),
            device_id_type=MESH,
        )
        return 0

    lax.fori_loop(1, group, greet, 0)
    for n in range(1, peers):
        pl.semaphore_signal(
            barrier,
            inc=1,
            device_id=(lax.rem(p + n, peers) * CORES + c, g),
            device_id_type=MESH,
        )
    pl.semaphore_wait(barrier, group - 1 + peers - 1)

    def blocks_of(k, origin, sub):
        return bufs[k].at[c, pl.ds(origin * bd + sub * sub_n, sub_n)]

    def ring_copy(way, s, k, sub):
        origin = ring_at(pos - (s - 1)) if way == 0 else ring_at(pos + (s - 1))
        ref = blocks_of(k, origin, sub)
        return pltpu.make_async_remote_copy(
            src_ref=ref,
            dst_ref=ref,
            send_sem=ring_send.at[way, s - 1, k, sub],
            recv_sem=ring_recv.at[way, s - 1, k, sub],
            device_id=right if way == 0 else left,
            device_id_type=MESH,
        )

    def ring_arrival(way, s, k, sub):
        origin = ring_at(pos - s) if way == 0 else ring_at(pos + s)
        ref = blocks_of(k, origin, sub)
        return pltpu.make_async_remote_copy(
            src_ref=ref,
            dst_ref=ref,
            send_sem=ring_send.at[way, s - 1, k, sub],
            recv_sem=ring_recv.at[way, s - 1, k, sub],
            device_id=right if way == 0 else left,
            device_id_type=MESH,
        )

    def in_step(way, s, sub):
        return s < half_ring or (s == half_ring and way == sub // (subs // 2))

    def core_copy(way, s, k, sub, mine):
        origin = g if s == 0 else (ring_at(pos - s) if way == 0 else ring_at(pos + s))
        who = c if mine else 1 - c
        ref = bufs[k].at[who, pl.ds(origin * bd + sub * sub_n, sub_n)]
        if s == 0:
            sems = own_send.at[k, sub], own_recv.at[k, sub]
        else:
            sems = core_send.at[way, s - 1, k, sub], core_recv.at[way, s - 1, k, sub]
        return pltpu.make_async_remote_copy(
            src_ref=ref,
            dst_ref=ref,
            send_sem=sems[0],
            recv_sem=sems[1],
            device_id=sib,
            device_id_type=MESH,
        )

    def start_own(k):
        for sub in range(subs):
            for way in range(2):
                if in_step(way, 1, sub):
                    ring_copy(way, 1, k, sub).start()
        for sub in range(subs):
            core_copy(0, 0, k, sub, True).start()

    def serve(k, s):
        for sub in range(subs):
            for way in range(2):
                if not in_step(way, s, sub):
                    continue
                ring_arrival(way, s, k, sub).wait_recv()
                if in_step(way, s + 1, sub):
                    ring_copy(way, s + 1, k, sub).start()
                core_copy(way, s, k, sub, True).start()

    def core_arrivals(k):
        for sub in range(subs):
            core_copy(0, 0, k, sub, False).wait_recv()
            for s in range(1, half_ring + 1):
                for way in range(2):
                    if in_step(way, s, sub):
                        core_copy(way, s, k, sub, False).wait_recv()

    for copy in tok_copies:
        copy.wait()
    start_own(0)

    for copy in small_copies:
        copy.wait()
    row = jnp.broadcast_to(seq_ref[...].astype(F32), (T, T))
    same = (row == row.T).astype(F32)
    tok_weight = T / (SEGS * jnp.sum(same, axis=1, keepdims=True))
    cot_copy.wait()
    for b in range(bd):
        cotb[c, g * bd + b] = (
            stage[:, b * B : (b + 1) * B].astype(F32) * tok_weight
        ).astype(BF16)

    for s in range(1, half_ring + 1):
        if s == max(1, half_ring - 1):
            start_own(1)
        serve(0, s)
    core_arrivals(0)
    for copy in w_copies:
        copy.wait()

    def forward(h, _):
        wcat = jnp.concatenate([og[h0 + h], ou[h0 + h]], axis=1)
        gain = unit_ref[pl.ds(h0 + h, 1), :]
        for r in range(CORES):
            x = jnp.concatenate([tokb[r, inb_ref[l, h0 + h]] for l in range(L)], axis=1)
            x_t[h, r] = x.T
            pre = jnp.dot(x, wcat, preferred_element_type=F32) * in_scale
            gate, up = pre[:, :B], pre[:, B:]
            sig = 1.0 / (1.0 + jnp.exp(-gate))
            silu = gate * sig
            hid_t[h, r] = (silu * up * gain).astype(BF16).T
            fac[h, r, :, :B] = gain * up * (sig * (1.0 + gate * (1.0 - sig))) * out_scale
            fac[h, r, :, B:] = gain * silu * out_scale
        return 0

    for s in range(1, half_ring + 1):
        serve(1, s)
        lo, hi = (s - 1) * hh // half_ring, s * hh // half_ring
        if hi > lo:
            lax.fori_loop(lo, hi, forward, 0)
    core_arrivals(1)

    def backward(h, sums):
        return backward_one(h * 2 + 1, backward_one(h * 2, sums)) if hh % 2 == 0 else backward_one(h, sums)

    def backward_one(h, sums):
        wd = jnp.concatenate([od[h0 + h, l * B : (l + 1) * B] for l in range(L)], axis=1)
        new = []
        for r in range(CORES):
            y = jnp.concatenate([cotb[r, outb_ref[l, h0 + h]] for l in range(L)], axis=1)
            dh = lax.dot_general(y, wd, (((1,), (1,)), ((), ())), preferred_element_type=F32)
            both = (jnp.concatenate([dh, dh], axis=1) * fac[h, r]).astype(BF16)
            down = jnp.dot(hid_t[h, r], y, preferred_element_type=F32)
            gdn[r, h] = down
            grad = jnp.dot(x_t[h, r], both, preferred_element_type=F32)
            ggu[r, h] = grad
            sq_in = jnp.sum((grad * grad).reshape(L * B // 8, 8, 2 * B), axis=0)
            sq_out = jnp.sum((down * down).reshape(B // 8, 8, L * B), axis=0)
            part = (sq_in[:, :B] + sq_in[:, B:]) * (in_scale * in_scale)
            for l in range(L):
                part = part + sq_out[:, l * B : (l + 1) * B] * (out_scale * out_scale)
            new.append(sums[r] + part)
        return tuple(new)

    zero = jnp.zeros((8, B), F32)
    sums = backward_one(0, (zero, zero))

    def early_copy(which, n, mine):
        ref = (eb, stb)[which].at[p if mine else lax.rem(p - n + peers, peers)]
        return pltpu.make_async_remote_copy(
            src_ref=ref,
            dst_ref=ref,
            send_sem=early_send.at[which, n - 1],
            recv_sem=early_recv.at[which, n - 1],
            device_id=(lax.rem(p + n, peers) * CORES + c, g),
            device_id_type=MESH,
        )

    for r in range(CORES):
        eb[p, r] = ggu[r, 0, :, :B].astype(BF16)
    for n in range(1, peers):
        early_copy(0, n, True).start()
    if hh % 2 == 0:
        sums = backward_one(1, sums)
    sums = lax.fori_loop(1, hh // 2 if hh % 2 == 0 else hh, backward, sums)
    for r in range(CORES):
        sqb[lin, r] = sums[r]

    def sq_copy(n, mine):
        other = lax.rem(lin + n, group)
        ref = sqb.at[lin if mine else lax.rem(lin - n + group, group)]
        return pltpu.make_async_remote_copy(
            src_ref=ref,
            dst_ref=ref,
            send_sem=sq_send.at[n - 1],
            recv_sem=sq_recv.at[n - 1],
            device_id=(p * CORES + lax.rem(other, CORES), other // CORES),
            device_id_type=MESH,
        )

    def sq_start(n, _):
        sq_copy(n, True).start()
        return 0

    def sq_wait(n, _):
        sq_copy(n, False).wait_recv()
        return 0

    lax.fori_loop(1, group, sq_start, 0)
    lax.fori_loop(1, group, sq_wait, 0)
    steps = []
    for r in range(CORES):
        total = jnp.sum(sqb[:, r], axis=0)
        total = jnp.sum(jnp.sum(total, axis=1, keepdims=True), axis=0, keepdims=True)
        rms = jnp.sqrt(total / count_all + 1e-06)
        steps.append(-LEARN_RATE * jnp.minimum(1.0, MAX_RMS / rms))

    for r in range(CORES):
        stb[p, r] = jnp.broadcast_to(steps[r] * in_scale, (8, B))
    for n in range(1, peers):
        early_copy(1, n, True).start()

    def x_copy(h, j, n, mine):
        ref = xb.at[p if mine else lax.rem(p - n + peers, peers), h, j]
        return pltpu.make_async_remote_copy(
            src_ref=ref,
            dst_ref=ref,
            send_sem=x_send.at[n - 1, h, j],
            recv_sem=x_recv.at[n - 1, h, j],
            device_id=(lax.rem(p + n, peers) * CORES + c, g),
            device_id_type=MESH,
        )

    def deltas(h, first):
        gu = ggu[0, h] * (steps[0] * in_scale) + ggu[1, h] * (steps[1] * in_scale)
        for j in range(1 if first else 0, 2):
            xb[p, h, j] = gu[:, j * B : (j + 1) * B].astype(BF16)
            for n in range(1, peers):
                x_copy(h, j, n, True).start()
        dn = gdn[0, h] * (steps[0] * out_scale) + gdn[1, h] * (steps[1] * out_scale)
        for l in range(L):
            xb[p, h, 2, l * B : (l + 1) * B] = dn[:, l * B : (l + 1) * B].astype(BF16)
        for n in range(1, peers):
            x_copy(h, 2, n, True).start()

    def deltas_step(h, _):
        deltas(h, False)
        return 0

    deltas(0, True)
    lax.fori_loop(1, hh, deltas_step, 0)

    def out_copy(h, j, mine):
        ref = outs[j].at[(h0 if mine else (1 - c) * hh) + h]
        return pltpu.make_async_remote_copy(
            src_ref=ref,
            dst_ref=ref,
            send_sem=out_send.at[j, h],
            recv_sem=out_recv.at[j, h],
            device_id=sib,
            device_id_type=MESH,
        )

    def update(h, first):
        for j in range(3):
            if first and j == 0:
                for n in range(1, peers):
                    early_copy(0, n, False).wait_recv()
                    early_copy(1, n, False).wait_recv()
                total = jnp.zeros((L * B, B), F32)
                for q in range(peers):
                    for r in range(CORES):
                        total = total + stb[q, r, 0:1] * eb[q, r].astype(F32)
            else:
                for n in range(1, peers):
                    x_copy(h, j, n, False).wait_recv()
                total = xb[0, h, j].astype(F32)
                for q in range(1, peers):
                    total = total + xb[q, h, j].astype(F32)
            new = outs[j][h0 + h].astype(F32) + total * (1.0 / R)
            outs[j][h0 + h] = new.astype(BF16)
            out_copy(h, j, True).start()

    def update_step(h, _):
        update(h, False)
        return 0

    update(0, True)
    lax.fori_loop(1, hh, update_step, 0)

    for k in range(2):
        for sub in range(subs):
            core_copy(0, 0, k, sub, True).wait_send()
            for s in range(1, half_ring + 1):
                for way in range(2):
                    if in_step(way, s, sub):
                        ring_copy(way, s, k, sub).wait_send()
                        core_copy(way, s, k, sub, True).wait_send()

    def sq_sent(n, _):
        sq_copy(n, True).wait_send()
        return 0

    lax.fori_loop(1, group, sq_sent, 0)

    def finish(h, first):
        for j in range(3):
            for n in range(1, peers):
                if first and j == 0:
                    early_copy(0, n, True).wait_send()
                    early_copy(1, n, True).wait_send()
                else:
                    x_copy(h, j, n, True).wait_send()
            out_copy(h, j, True).wait_send()
            out_copy(h, j, False).wait_recv()

    def finish_step(h, _):
        finish(h, False)
        return 0

    finish(0, True)
    lax.fori_loop(1, hh, finish_step, 0)


def store_kernel(a, b, c, out_a, out_b, out_c, sems):
    copies = [
        pltpu.make_async_copy(src, dst, sems.at[j])
        for j, (src, dst) in enumerate(((a, out_a), (b, out_b), (c, out_c)))
    ]
    for copy in copies:
        copy.start()
    for copy in copies:
        copy.wait()


def per_device(
    G, R, tokens, cotangent, seq_ids, in_blocks, out_blocks, unit_scale, gate_w, up_w, down_w
):
    T, width = tokens.shape
    hb, L, B, _ = gate_w.shape
    bd = width // B
    nb, ff, d_model = bd * G, hb * G * B, width * G
    hh, peers, half = hb // CORES, R // CORES, G // 2
    subs = 4 if bd % 4 == 0 else 2
    cfg = dict(
        G=G,
        R=R,
        T=T,
        bd=bd,
        hb=hb,
        subs=subs,
        L=L,
        B=B,
        in_scale=float((L * B) ** -0.5),
        out_scale=float((L * B * (ff // d_model)) ** -0.5),
        count_all=float(3 * hb * G * L * B * B),
    )
    flat = lambda w: w.reshape(hb, L * B, B)
    any_spec = pl.BlockSpec(memory_space=pl.ANY)
    dma = pltpu.SemaphoreType.DMA
    outs = pl.pallas_call(
        functools.partial(kernel, cfg),
        out_shape=[pltpu.VMEM((hb, L * B, B), BF16)] * 3,
        in_specs=[any_spec] * 9,
        out_specs=[pl.BlockSpec(memory_space=pltpu.VMEM)] * 3,
        scratch_shapes=[
            pltpu.VMEM((CORES, nb, T, B), BF16),
            pltpu.VMEM((CORES, nb, T, B), BF16),
            pltpu.VMEM((T, width), BF16),
            pltpu.VMEM((hh, CORES, T, 2 * B), F32),
            pltpu.VMEM((hh, CORES, B, T), BF16),
            pltpu.VMEM((hh, CORES, L * B, T), BF16),
            pltpu.VMEM((CORES, hh, L * B, 2 * B), F32),
            pltpu.VMEM((CORES, hh, B, L * B), F32),
            pltpu.VMEM((peers, hh, 3, L * B, B), BF16),
            pltpu.VMEM((G * CORES, CORES, 8, B), F32),
            pltpu.VMEM((peers, CORES, L * B, B), BF16),
            pltpu.VMEM((peers, CORES, 8, B), F32),
            dma((2, peers - 1)),
            dma((2, peers - 1)),
            pltpu.VMEM((1, T), jnp.int32),
            pltpu.VMEM((hb, B), F32),
            pltpu.SMEM((L, hb), jnp.int32),
            pltpu.SMEM((L, hb), jnp.int32),
            dma((4,)),
            dma((bd,)),
            dma,
            dma((3,)),
            dma((2, half, 2, subs)),
            dma((2, half, 2, subs)),
            dma((2, subs)),
            dma((2, subs)),
            dma((2, half, 2, subs)),
            dma((2, half, 2, subs)),
            dma((G * CORES - 1,)),
            dma((G * CORES - 1,)),
            dma((peers - 1, hh, 3)),
            dma((peers - 1, hh, 3)),
            dma((3, hh)),
            dma((3, hh)),
        ],
        compiler_params=pltpu.CompilerParams(
            collective_id=0, has_side_effects=True, vmem_limit_bytes=56 * 1024 * 1024
        ),
    )(
        tokens,
        cotangent,
        seq_ids,
        in_blocks.T,
        out_blocks.T,
        unit_scale.reshape(hb, B),
        flat(gate_w),
        flat(up_w),
        flat(down_w),
    )
    outs = pl.pallas_call(
        store_kernel,
        out_shape=[jax.ShapeDtypeStruct((hb, L * B, B), BF16)] * 3,
        in_specs=[any_spec] * 3,
        out_specs=[any_spec] * 3,
        scratch_shapes=[dma((3,))],
        compiler_params=pltpu.CompilerParams(vmem_limit_bytes=1024 * 1024),
    )(*outs)
    return tuple(o.reshape(hb, L, B, B) for o in outs)


def solution(mesh):
    return jax.shard_map(
        functools.partial(per_device, mesh.shape["hid"], mesh.shape["rep"]),
        mesh=mesh,
        in_specs=(
            P("rep", "hid"),
            P("rep", "hid"),
            P("rep", None),
            P("hid", None),
            P("hid", None),
            P("hid"),
            P("hid", None, None, None),
            P("hid", None, None, None),
            P("hid", None, None, None),
        ),
        out_specs=(
            P("hid", None, None, None),
            P("hid", None, None, None),
            P("hid", None, None, None),
        ),
        check_vma=False,
    )
```
